32 devices in a mesh: seq: 16 (over z, x, core), tp: 2 (over y).
Axes of the slice: x: 2, y: 2, z: 4, core: 2. Of those that a mesh axis runs over, the one named last changes fastest.
Arguments:
- latents: bfloat16 [4096, 3072], P('seq', 'tp'), may hold values from -16 to 16
- noise: bfloat16 [4096, 3072], P('seq', 'tp'), may hold values from -16 to 16
- timestep: int32 [1], replicated, may hold values from 1 to 1000
- text_len: int32 [1], replicated, may hold values from 64 to 256
- text_kv: bfloat16 [2, 256, 3072], P(None, None, 'tp'), may hold values from -32 to 32
- norm_gain: float32 [3072], replicated, may hold values from 0.1 to 1.9
- w_qkv: bfloat16 [3072, 3, 3072], P(None, None, 'tp')
- qk_gain: float32 [2, 128], replicated, may hold values from 0.1 to 1.9
- w_out: bfloat16 [3072, 3072], P('tp'), may hold values from -3 to 3
- out_gate: float32 [3072], P('tp'), may hold values from 0.5 to 1.5
Outputs:
- prediction: bfloat16 [4096, 3072], P('seq', 'tp')
- loss: float32 [], replicated
The draws below stay inside these ranges and needn't reach their ends.
All inputs are finite; a program needn't handle non-finite values.
Results may differ from the reference program's by a relative error of at most 0.014.
Values may be sent and summed in bfloat16 or wider, within the bound.
A program may use at most 192 MiB of HBM per device.

```python
import jax
import jax.numpy as jnp
from jax import lax

D = 3072
HEADS = 24
HD = 128
TXT = 256
TOKENS = 4096


def token_field(key, salt):
    base = jax.random.normal(jax.random.fold_in(key, salt), (TOKENS, D), jnp.float32)
    place = jnp.arange(TOKENS, dtype=jnp.float32) / jnp.float32(TOKENS - 1)
    rising = 1.0 + 2.0 * place
    base = base * rising[:, None]
    return jnp.clip(base, -16.0, 16.0).astype(jnp.bfloat16)


def draw_latents(key, part):
    return token_field(key, 11)


def draw_noise(key, part):
    return token_field(key, 12)


def draw_w_qkv(key, part):
    base = jax.random.normal(jax.random.fold_in(key, 13), (D, 3, HEADS * HD), jnp.float32)
    base = jnp.clip(base, -6.0, 6.0) / jnp.sqrt(jnp.float32(D))
    return base.astype(jnp.bfloat16)


def draw_text_kv(key, part):
    base = jax.random.normal(jax.random.fold_in(key, 14), (2, TXT, HEADS * HD), jnp.float32)
    base = jnp.clip(base, -6.0, 6.0)
    return base.astype(jnp.bfloat16)


def level_of(stream_key, dims, pieces, least, high):
    level = 1.0
    for axis_at, shards_of in pieces:
        heights = jax.random.uniform(jax.random.fold_in(jax.random.fold_in(stream_key, 6), axis_at), (shards_of,), jnp.float32, least / len(pieces), high / len(pieces))
        level = level * jnp.repeat(jnp.exp(heights), dims[axis_at] // shards_of).reshape((-1,) + (1,) * (len(dims) - 1 - axis_at))
    return level


def gaussian(rng, shape, deviation, limit, split=(), kind=jnp.bfloat16):
    entries = deviation * jax.random.normal(rng, shape, jnp.float32)
    if split:
        entries = entries * level_of(rng, shape, split, -0.22, 0.18)
    return jnp.clip(entries, -limit, limit).astype(kind)


def setup_inputs(seed: int = 0) -> dict:
    seeds = jax.random.split(jax.random.key(seed), 11)
    latents = draw_latents(jax.random.fold_in(seeds[10], 71), 0)
    noise = draw_noise(jax.random.fold_in(seeds[10], 71), 0)
    timestep = jax.random.randint(seeds[2], (1,), 1, 1001).astype(jnp.int32)
    text_len = jax.random.randint(seeds[3], (1,), TXT // 4, TXT + 1).astype(jnp.int32)
    text_kv = draw_text_kv(jax.random.fold_in(seeds[10], 71), 0)
    norm_gain = jnp.clip(1.0 + 0.18 * jax.random.normal(seeds[5], (D,), jnp.float32), 0.1, 1.9)
    w_qkv = draw_w_qkv(jax.random.fold_in(seeds[10], 71), 0)
    qk_gain = jnp.clip(1.0 + 0.18 * jax.random.normal(seeds[7], (2, HD), jnp.float32), 0.1, 1.9)
    w_out = gaussian(seeds[8], (HEADS * HD, D), 0.5, 3.0, ((0, 2),))
    out_gate = jnp.clip(0.5 + 1.0 * jax.random.uniform(seeds[9], (D,), jnp.float32) ** level_of(seeds[9], (D,), ((0, 2),), -0.2, 0.2), 0.5, 1.5)
    return {"latents": latents, "noise": noise, "timestep": timestep, "text_len": text_len, "text_kv": text_kv, "norm_gain": norm_gain, "w_qkv": w_qkv, "qk_gain": qk_gain, "w_out": w_out, "out_gate": out_gate}


def reference(latents, noise, timestep, text_len, text_kv, norm_gain, w_qkv, qk_gain, w_out, out_gate):
    sigma = timestep[0].astype(jnp.float32) / 1000.0
    noisy = (1.0 - sigma) * latents.astype(jnp.float32) + sigma * noise.astype(jnp.float32)
    center = noisy - lax.optimization_barrier(jnp.mean(noisy, axis=-1, keepdims=True))
    spread = lax.optimization_barrier(jnp.mean(center * center, axis=-1, keepdims=True))
    normed = (center * lax.rsqrt(spread + 1e-06) * norm_gain).astype(jnp.bfloat16)
    width = HEADS * HD
    qkv = jnp.dot(normed, w_qkv.reshape(D, 3 * width), preferred_element_type=jnp.float32)
    qkv = qkv.reshape(TOKENS, 3, HEADS, HD)

    def qknorm(block, gain):
        return (block * lax.rsqrt(lax.optimization_barrier(jnp.mean(block * block, axis=-1, keepdims=True)) + 1e-06) * gain).astype(jnp.bfloat16)
    query = qknorm(qkv[:, 0], qk_gain[0])
    key = qknorm(qkv[:, 1], qk_gain[1])
    value = qkv[:, 2].astype(jnp.bfloat16)
    text_keys = text_kv[0].reshape(TXT, HEADS, HD)
    text_vals = text_kv[1].reshape(TXT, HEADS, HD)
    valid = jnp.concatenate([jnp.arange(TXT, dtype=jnp.int32) < text_len[0], jnp.ones((TOKENS,), bool)])

    def per_head(head):
        qh = lax.dynamic_index_in_dim(query, head, 1, False)
        keys = jnp.concatenate([lax.dynamic_index_in_dim(text_keys, head, 1, False), lax.dynamic_index_in_dim(key, head, 1, False)], 0)
        vals = jnp.concatenate([lax.dynamic_index_in_dim(text_vals, head, 1, False), lax.dynamic_index_in_dim(value, head, 1, False)], 0)
        scores = jnp.dot(qh, keys.T, preferred_element_type=jnp.float32) / jnp.sqrt(jnp.float32(HD))
        scores = jnp.where(valid[None, :], scores, -jnp.inf)
        weights = jax.nn.softmax(scores, axis=-1).astype(jnp.bfloat16)
        return jnp.dot(weights, vals, preferred_element_type=jnp.float32).astype(jnp.bfloat16)
    heads_out = lax.map(per_head, jnp.arange(HEADS, dtype=jnp.int32))
    attended = jnp.transpose(heads_out, (1, 0, 2)).reshape(TOKENS, width)
    mixed = jnp.dot(attended, w_out, preferred_element_type=jnp.float32)
    prediction = (noisy + out_gate * mixed).astype(jnp.bfloat16)
    target = noise.astype(jnp.float32) - latents.astype(jnp.float32)
    error = prediction.astype(jnp.float32) - target
    loss = jnp.mean(error * error)
    return (prediction, loss)
```

```python
import functools

import jax
import jax.numpy as jnp
from jax import lax
from jax.experimental import pallas as pl
from jax.experimental.pallas import tpu as pltpu
from jax.sharding import PartitionSpec as P

HD = 128
MESH = pl.DeviceIdType.MESH
ANY = pl.BlockSpec(memory_space=pl.ANY)
LOG2E = 1.4426950408889634


def project_kernel(x_ref, w_ref, gain_ref, out_ref):
    part = pl.program_id(0)
    y = jnp.dot(x_ref[...], w_ref[0], preferred_element_type=jnp.float32)
    gain = gain_ref[0]
    for h in range(y.shape[1] // HD):
        block = y[:, h * HD : (h + 1) * HD]
        scale = lax.rsqrt(jnp.mean(block * block, axis=-1, keepdims=True) + 1e-06)
        scale = jnp.where(part < 2, scale, 1.0)
        out_ref[0, 0, :, h * HD : (h + 1) * HD] = (block * scale * gain).astype(jnp.bfloat16)


def project(normed, w, gains, groups):
    rows, depth = normed.shape
    width = w.shape[2] // groups
    return pl.pallas_call(
        project_kernel,
        grid=(3, groups),
        in_specs=[
            pl.BlockSpec((rows, depth), lambda s, g: (0, 0)),
            pl.BlockSpec((1, depth, width), lambda s, g: (s, 0, g)),
            pl.BlockSpec((1, 1, HD), lambda s, g: (s, 0, 0)),
        ],
        out_specs=pl.BlockSpec((1, 1, rows, width), lambda s, g: (s, g, 0, 0)),
        out_shape=jax.ShapeDtypeStruct((3, groups, rows, width), jnp.bfloat16),
        compiler_params=pltpu.CompilerParams(vmem_limit_bytes=40 << 20),
    )(normed, w, gains)


def greet(peers):
    barrier = pltpu.get_barrier_semaphore()
    for peer in peers:
        pl.semaphore_signal(barrier, inc=1, device_id={"seq": peer}, device_id_type=MESH)
    pl.semaphore_wait(barrier, len(peers))


def remote(src, dst, send, recv, peer):
    return pltpu.make_async_remote_copy(
        src_ref=src, dst_ref=dst, send_sem=send, recv_sem=recv,
        device_id={"seq": peer}, device_id_type=MESH,
    )


def deal_kernel(groups, inner, qkv, q_all, kv_all, zs, zr, qs, qr, xs, xr, cs, cr, fs, fr, ls):
    me = lax.axis_index("seq")
    j = lax.rem(me, inner)
    z = me // inner
    core = lax.rem(j, 2)
    x = j // 2
    xj = (1 - x) * 2 + core
    cj = x * 2 + (1 - core)
    x_mate = z * inner + xj
    c_mate = z * inner + cj
    order = [2, 1, 3]
    peers = {k: lax.rem(z + k, groups) * inner + j for k in order}
    greet([peers[k] for k in order] + [x_mate, c_mate])
    waits = []
    firsts = {}
    for k in order:
        to = lax.rem(z + k, groups)
        firsts[k] = remote(
            qkv.at[pl.ds(1, 2), to], kv_all.at[:, z, j], zs.at[k - 1], zr.at[k - 1], peers[k]
        )
        firsts[k].start()
    own_kv = pltpu.make_async_copy(qkv.at[pl.ds(1, 2), z], kv_all.at[:, z, j], ls.at[0])
    own_q = pltpu.make_async_copy(qkv.at[0, z], q_all.at[z], ls.at[1])
    own_kv.start()
    own_q.start()
    by_x = {}
    by_c = {}
    quers = {}
    for k in [0] + order:
        at = lax.rem(z + groups - k, groups)
        if k == 0:
            src = qkv.at[pl.ds(1, 2), z]
        else:
            firsts[k].wait_recv()
            src = kv_all.at[:, at, j]
        by_x[k] = remote(src, kv_all.at[:, at, j], xs.at[k], xr.at[k], x_mate)
        by_x[k].start()
        by_c[k] = remote(src, kv_all.at[:, at, j], cs.at[k], cr.at[k], c_mate)
        by_c[k].start()
        if k == 0:
            for m in order:
                to = lax.rem(z + m, groups)
                quers[m] = remote(
                    qkv.at[0, to], q_all.at[z], qs.at[m - 1], qr.at[m - 1], peers[m]
                )
                quers[m].start()
    passed = {}
    for k in [0] + order:
        at = lax.rem(z + groups - k, groups)
        by_x[k].wait_recv()
        passed[k] = remote(
            kv_all.at[:, at, xj], kv_all.at[:, at, xj], fs.at[k], fr.at[k], c_mate
        )
        passed[k].start()
    own_kv.wait()
    own_q.wait()
    for k in order:
        firsts[k].wait_send()
        quers[k].wait()
    for k in [0] + order:
        by_x[k].wait_send()
        by_c[k].wait()
        passed[k].wait()


def deal(qkv, inner):
    _, groups, rows, width = qkv.shape
    dma = pltpu.SemaphoreType.DMA
    return pl.pallas_call(
        functools.partial(deal_kernel, groups, inner),
        in_specs=[ANY],
        out_specs=[ANY, ANY],
        out_shape=[
            jax.ShapeDtypeStruct((groups, rows, width), jnp.bfloat16),
            jax.ShapeDtypeStruct((2, groups, inner, rows, width), jnp.bfloat16),
        ],
        scratch_shapes=[dma((3,)), dma((3,)), dma((3,)), dma((3,))]
        + [dma((4,)) for _ in range(6)]
        + [dma((2,))],
        compiler_params=pltpu.CompilerParams(collective_id=1, has_side_effects=True),
    )(qkv)


def back_kernel(groups, inner, o_ref, out_ref, ss, rs, ls):
    me = lax.axis_index("seq")
    j = lax.rem(me, inner)
    z = me // inner
    order = [2, 1, 3]
    peers = {k: lax.rem(z + k, groups) * inner + j for k in order}
    greet([peers[k] for k in order])
    copies = []
    for k in order:
        to = lax.rem(z + k, groups)
        copies.append(
            remote(o_ref.at[to], out_ref.at[z], ss.at[k - 1], rs.at[k - 1], peers[k])
        )
        copies[-1].start()
    own = pltpu.make_async_copy(o_ref.at[z], out_ref.at[z], ls.at[0])
    own.start()
    own.wait()
    for copy in copies:
        copy.wait()


def back(o, inner):
    dma = pltpu.SemaphoreType.DMA
    return pl.pallas_call(
        functools.partial(back_kernel, o.shape[0], inner),
        in_specs=[ANY],
        out_specs=ANY,
        out_shape=jax.ShapeDtypeStruct(o.shape, jnp.bfloat16),
        scratch_shapes=[dma((3,)), dma((3,)), dma((1,))],
        compiler_params=pltpu.CompilerParams(collective_id=2, has_side_effects=True),
    )(o)


def attend_kernel(len_ref, q_ref, kv_ref, text_ref, out_ref):
    zq, rows, _ = q_ref.shape
    q = q_ref[...].reshape(zq * rows, HD)
    nt = (((1,), (1,)), ((), ()))
    text = text_ref.shape[1]
    ones = jnp.ones((text, HD), jnp.bfloat16)
    st = lax.dot_general(q, text_ref[0], nt, preferred_element_type=jnp.float32)
    ok = lax.broadcasted_iota(jnp.int32, st.shape, 1) < len_ref[0]
    st = jnp.where(ok, st, -1e30)
    top = jnp.maximum(jnp.max(st, axis=-1, keepdims=True), 0.0)
    pt = jnp.exp2(st - top).astype(jnp.bfloat16)
    acc_t = jnp.dot(
        pt, jnp.concatenate([text_ref[1], ones], axis=1), preferred_element_type=jnp.float32
    )
    _, groups, inner, keys, _ = kv_ref.shape
    ones = jnp.ones((2 * keys, HD), jnp.bfloat16)
    acc = jnp.zeros((zq * rows, 2 * HD), jnp.float32)
    for g in range(groups):
        for i in range(0, inner, 2):
            k = kv_ref[0, g, i : i + 2].reshape(2 * keys, HD)
            v = kv_ref[1, g, i : i + 2].reshape(2 * keys, HD)
            s = lax.dot_general(q, k, nt, preferred_element_type=jnp.float32)
            p = jnp.exp2(s).astype(jnp.bfloat16)
            acc += jnp.dot(
                p, jnp.concatenate([v, ones], axis=1), preferred_element_type=jnp.float32
            )
    acc = acc * jnp.exp2(-top) + acc_t
    out = acc[:, :HD] / acc[:, HD:]
    out_ref[...] = out.astype(jnp.bfloat16).reshape(zq, rows, HD)


def attend(text_len, q_all, kv_all, text):
    qg, rows, width = q_all.shape
    _, groups, inner, keys, _ = kv_all.shape
    step = 2 if qg % 2 == 0 else 1
    return pl.pallas_call(
        attend_kernel,
        grid=(width // HD, qg // step),
        in_specs=[
            pl.BlockSpec(memory_space=pltpu.SMEM),
            pl.BlockSpec((step, rows, HD), lambda h, b: (b, 0, h)),
            pl.BlockSpec((2, groups, inner, keys, HD), lambda h, b: (0, 0, 0, 0, h)),
            pl.BlockSpec((2, text.shape[1], HD), lambda h, b: (0, 0, h)),
        ],
        out_specs=pl.BlockSpec((step, rows, HD), lambda h, b: (b, 0, h)),
        out_shape=jax.ShapeDtypeStruct(q_all.shape, jnp.bfloat16),
        compiler_params=pltpu.CompilerParams(vmem_limit_bytes=48 << 20),
    )(text_len, q_all, kv_all, text)


def total_kernel(sizes, in_ref, out_ref, held, ss, rs):
    places = []
    for axis, size in sizes:
        me = lax.axis_index(axis)
        bit = 1
        while bit < size:
            low = lax.rem(me // bit, 2)
            places.append((axis, me + bit - 2 * bit * low))
            bit *= 2
    barrier = pltpu.get_barrier_semaphore()
    for axis, peer in places:
        pl.semaphore_signal(barrier, inc=1, device_id={axis: peer}, device_id_type=MESH)
    pl.semaphore_wait(barrier, len(places))
    out_ref[...] = in_ref[...]
    for n, (axis, peer) in enumerate(places):
        held[n, 0] = out_ref[...]
        copy = pltpu.make_async_remote_copy(
            src_ref=held.at[n, 0], dst_ref=held.at[n, 1], send_sem=ss.at[n], recv_sem=rs.at[n],
            device_id={axis: peer}, device_id_type=MESH,
        )
        copy.start()
        copy.wait()
        out_ref[...] = held[n, 0] + held[n, 1]


def total(value):
    sizes = (("seq", lax.axis_size("seq")), ("tp", lax.axis_size("tp")))
    steps = sum(size.bit_length() - 1 for _, size in sizes)
    dma = pltpu.SemaphoreType.DMA
    vmem = pl.BlockSpec(memory_space=pltpu.VMEM)
    full = jnp.broadcast_to(value, (8, 128))
    return pl.pallas_call(
        functools.partial(total_kernel, sizes),
        in_specs=[vmem],
        out_specs=vmem,
        out_shape=jax.ShapeDtypeStruct((8, 128), jnp.float32),
        scratch_shapes=[pltpu.VMEM((steps, 2, 8, 128), jnp.float32), dma((steps,)), dma((steps,))],
        compiler_params=pltpu.CompilerParams(collective_id=3, has_side_effects=True),
    )(full)[0, 0]


def shards(latents, noise, timestep, text_len, text_kv, norm_gain, w_qkv, qk_gain, w_out, out_gate):
    rows, local_width = latents.shape
    seq, tp = lax.axis_size("seq"), lax.axis_size("tp")
    at_seq, at_tp = lax.axis_index("seq"), lax.axis_index("tp")
    head_width = w_qkv.shape[2]
    heads_dev = head_width // HD
    groups = 4 if seq == 16 and heads_dev % 4 == 0 else 1
    inner = seq // groups
    width = head_width // groups

    sigma = timestep[0].astype(jnp.float32) / 1000.0
    noisy = (1.0 - sigma) * latents.astype(jnp.float32) + sigma * noise.astype(jnp.float32)
    sent = noisy.astype(jnp.bfloat16)
    if tp == 2:
        other = lax.ppermute(sent, "tp", [(0, 1), (1, 0)])
        first = jnp.where(at_tp == 0, sent, other)
        second = jnp.where(at_tp == 0, other, sent)
        full = jnp.concatenate([first, second], axis=1).astype(jnp.float32)
    else:
        full = lax.all_gather(sent, "tp", axis=1, tiled=True).astype(jnp.float32)
    center = full - jnp.mean(full, axis=-1, keepdims=True)
    spread = jnp.mean(center * center, axis=-1, keepdims=True)
    normed = (center * lax.rsqrt(spread + 1e-06) * norm_gain).astype(jnp.bfloat16)
    gains = jnp.stack(
        [qk_gain[0] * (LOG2E / HD**0.5), qk_gain[1], jnp.ones_like(qk_gain[0])]
    ).reshape(3, 1, HD)
    qkv = project(normed, jnp.transpose(w_qkv, (1, 0, 2)), gains, groups)
    if groups > 1:
        q_all, kv_all = deal(qkv, inner)
        text = lax.dynamic_slice_in_dim(text_kv, (at_seq // inner) * width, width, 2)
        attended = back(attend(text_len, q_all, kv_all, text), inner)
        attended = jnp.transpose(attended, (1, 0, 2)).reshape(rows, head_width)
    else:
        kv_all = lax.all_gather(qkv[1:, 0], "seq", axis=1)[:, None]
        attended = attend(text_len, qkv[0], kv_all, text_kv)[0]
    mixed = jnp.dot(attended, w_out, preferred_element_type=jnp.float32)
    if tp == 2:
        away = lax.dynamic_slice_in_dim(mixed, (1 - at_tp) * local_width, local_width, 1)
        away = lax.ppermute(away.astype(jnp.bfloat16), "tp", [(0, 1), (1, 0)])
        here = lax.dynamic_slice_in_dim(mixed, at_tp * local_width, local_width, 1)
        mixed = here + away.astype(jnp.float32)
    else:
        mixed = lax.psum_scatter(
            mixed.astype(jnp.bfloat16), "tp", scatter_dimension=1, tiled=True
        ).astype(jnp.float32)
    prediction = (noisy + out_gate * mixed).astype(jnp.bfloat16)
    target = noise.astype(jnp.float32) - latents.astype(jnp.float32)
    error = prediction.astype(jnp.float32) - target
    loss = total(jnp.sum(error * error)) / jnp.float32(rows * seq * local_width * tp)
    return (prediction, loss)


def solution(mesh):
    placed = (
        P("seq", "tp"),
        P("seq", "tp"),
        P(),
        P(),
        P(None, None, "tp"),
        P(),
        P(None, None, "tp"),
        P(),
        P("tp", None),
        P("tp"),
    )
    return jax.shard_map(
        shards, mesh=mesh, in_specs=placed, out_specs=(P("seq", "tp"), P()), check_vma=False
    )
```

```python
import functools

import jax
import jax.numpy as jnp
from jax import lax
from jax.experimental import pallas as pl
from jax.experimental.pallas import tpu as pltpu
from jax.sharding import PartitionSpec as P

HD = 128
MESH = pl.DeviceIdType.MESH
ANY = pl.BlockSpec(memory_space=pl.ANY)
LOG2E = 1.4426950408889634


def project_kernel(x_ref, w_ref, gain_ref, out_ref):
    part = pl.program_id(0)
    y = jnp.dot(x_ref[...], w_ref[0], preferred_element_type=jnp.float32)
    gain = gain_ref[0]
    for h in range(y.shape[1] // HD):
        block = y[:, h * HD : (h + 1) * HD]
        scale = lax.rsqrt(jnp.mean(block * block, axis=-1, keepdims=True) + 1e-06)
        scale = jnp.where(part < 2, scale, 1.0)
        out_ref[0, 0, :, h * HD : (h + 1) * HD] = (block * scale * gain).astype(jnp.bfloat16)


def project(normed, w, gains, groups):
    rows, depth = normed.shape
    width = w.shape[2] // groups
    return pl.pallas_call(
        project_kernel,
        grid=(3, groups),
        in_specs=[
            pl.BlockSpec((rows, depth), lambda s, g: (0, 0)),
            pl.BlockSpec((1, depth, width), lambda s, g: (s, 0, g)),
            pl.BlockSpec((1, 1, HD), lambda s, g: (s, 0, 0)),
        ],
        out_specs=pl.BlockSpec((1, 1, rows, width), lambda s, g: (s, g, 0, 0)),
        out_shape=jax.ShapeDtypeStruct((3, groups, rows, width), jnp.bfloat16),
        compiler_params=pltpu.CompilerParams(vmem_limit_bytes=40 << 20),
    )(normed, w, gains)


def greet(peers):
    barrier = pltpu.get_barrier_semaphore()
    for peer in peers:
        pl.semaphore_signal(barrier, inc=1, device_id={"seq": peer}, device_id_type=MESH)
    pl.semaphore_wait(barrier, len(peers))


def remote(src, dst, send, recv, peer):
    return pltpu.make_async_remote_copy(
        src_ref=src, dst_ref=dst, send_sem=send, recv_sem=recv,
        device_id={"seq": peer}, device_id_type=MESH,
    )


def group_at(i):
    return jnp.where(i == 3, 3, lax.rem(i + 1, 3))


def tile_at(t):
    keyed = t < 8
    return jnp.where(keyed, 1 + lax.rem(t, 2), 0), group_at(jnp.where(keyed, t // 2, t - 8))


def deal_kernel(
    groups, inner, x_ref, w_ref, gain_ref, q_all, kv_all,
    stage, zs, zr, xs, xr, cs, cr, fs, fr, ls,
):
    t = pl.program_id(0)
    part, to = tile_at(t)
    me = lax.axis_index("seq")
    j = lax.rem(me, inner)
    z = me // inner
    core = lax.rem(j, 2)
    x = j // 2
    xj = (1 - x) * 2 + core
    cj = x * 2 + (1 - core)
    x_mate = z * inner + xj
    c_mate = z * inner + cj

    @pl.when(t == 0)
    def _():
        greet([lax.rem(z + k, groups) * inner + j for k in range(1, groups)] + [x_mate, c_mate])

    y = jnp.dot(x_ref[...], w_ref[0], preferred_element_type=jnp.float32)
    gain = gain_ref[0]
    for h in range(y.shape[1] // HD):
        block = y[:, h * HD : (h + 1) * HD]
        scale = lax.rsqrt(jnp.mean(block * block, axis=-1, keepdims=True) + 1e-06)
        scale = jnp.where(part < 2, scale, 1.0)
        stage[part, to, :, h * HD : (h + 1) * HD] = (block * scale * gain).astype(jnp.bfloat16)

    def kv_copy(s, g, frm):
        return remote(
            stage.at[s, g], kv_all.at[s - 1, z if frm is None else frm, j], zs.at[s, g],
            zr.at[s, z if frm is None else frm], g * inner + j,
        )

    def q_copy(g, frm):
        return remote(
            stage.at[0, g], q_all.at[z if frm is None else frm], zs.at[0, g],
            zr.at[0, z if frm is None else frm], g * inner + j,
        )

    own_kv = pltpu.make_async_copy(stage.at[pl.ds(1, 2), z], kv_all.at[:, z, j], ls.at[0])
    own_q = pltpu.make_async_copy(stage.at[0, z], q_all.at[z], ls.at[1])

    @pl.when(jnp.logical_and(part > 0, to != z))
    def _():
        kv_copy(part, to, None).start()

    @pl.when(jnp.logical_and(part == 0, to != z))
    def _():
        q_copy(to, None).start()

    def spread(k):
        at = lax.rem(z + groups - k, groups)
        src = stage.at[pl.ds(1, 2), z] if k == 0 else kv_all.at[:, at, j]
        dst = kv_all.at[:, at, j]
        return (
            remote(src, dst, xs.at[k], xr.at[k], x_mate),
            remote(src, dst, cs.at[k], cr.at[k], c_mate),
        )

    @pl.when(t == 7)
    def _():
        own_kv.start()
        for copy in spread(0):
            copy.start()

    @pl.when(t == 11)
    def _():
        own_q.start()
        order = [1, 3, 2]
        for k in order:
            at = lax.rem(z + groups - k, groups)
            for s in (1, 2):
                kv_copy(s, at, at).wait_recv()
            for copy in spread(k):
                copy.start()
        passed = []
        for k in [0] + order:
            at = lax.rem(z + groups - k, groups)
            spread(k)[0].wait_recv()
            slot = kv_all.at[:, at, xj]
            passed.append(remote(slot, slot, fs.at[k], fr.at[k], c_mate))
            passed[-1].start()
        own_kv.wait()
        own_q.wait()
        for k in order:
            at = lax.rem(z + groups - k, groups)
            for s in (1, 2):
                kv_copy(s, at, at).wait_send()
            q_copy(at, at).wait()
        for k in range(groups):
            by_x, by_c = spread(k)
            by_x.wait_send()
            by_c.wait()
        for copy in passed:
            copy.wait()


def deal(normed, w, gains, groups, inner):
    rows, depth = normed.shape
    width = w.shape[2] // groups
    dma = pltpu.SemaphoreType.DMA
    return pl.pallas_call(
        functools.partial(deal_kernel, groups, inner),
        grid=(3 * groups,),
        in_specs=[
            pl.BlockSpec((rows, depth), lambda t: (0, 0)),
            pl.BlockSpec((1, depth, width), lambda t: (tile_at(t)[0], 0, tile_at(t)[1])),
            pl.BlockSpec((1, 1, HD), lambda t: (tile_at(t)[0], 0, 0)),
        ],
        out_specs=[ANY, ANY],
        out_shape=[
            jax.ShapeDtypeStruct((groups, rows, width), jnp.bfloat16),
            jax.ShapeDtypeStruct((2, groups, inner, rows, width), jnp.bfloat16),
        ],
        scratch_shapes=[
            pltpu.VMEM((3, groups, rows, width), jnp.bfloat16), dma((3, 4)), dma((3, 4)),
        ]
        + [dma((4,)) for _ in range(6)]
        + [dma((2,))],
        compiler_params=pltpu.CompilerParams(
            collective_id=1, has_side_effects=True, vmem_limit_bytes=40 << 20
        ),
    )(normed, w, gains)


def attention(len_ref, q_ref, kv_ref, text_ref):
    zq, rows, _ = q_ref.shape
    q = q_ref[...].reshape(zq * rows, HD)
    nt = (((1,), (1,)), ((), ()))
    text = text_ref.shape[1]
    ones = jnp.ones((text, HD), jnp.bfloat16)
    st = lax.dot_general(q, text_ref[0], nt, preferred_element_type=jnp.float32)
    ok = lax.broadcasted_iota(jnp.int32, st.shape, 1) < len_ref[0]
    st = jnp.where(ok, st, -1e30)
    top = jnp.maximum(jnp.max(st, axis=-1, keepdims=True), 0.0)
    pt = jnp.exp2(st - top).astype(jnp.bfloat16)
    acc_t = jnp.dot(
        pt, jnp.concatenate([text_ref[1], ones], axis=1), preferred_element_type=jnp.float32
    )
    _, groups, inner, keys, _ = kv_ref.shape
    ones = jnp.ones((2 * keys, HD), jnp.bfloat16)
    acc = jnp.zeros((zq * rows, 2 * HD), jnp.float32)
    for g in range(groups):
        for i in range(0, inner, 2):
            k = kv_ref[0, g, i : i + 2].reshape(2 * keys, HD)
            v = kv_ref[1, g, i : i + 2].reshape(2 * keys, HD)
            s = lax.dot_general(q, k, nt, preferred_element_type=jnp.float32)
            p = jnp.exp2(s).astype(jnp.bfloat16)
            acc += jnp.dot(
                p, jnp.concatenate([v, ones], axis=1), preferred_element_type=jnp.float32
            )
    acc = acc * jnp.exp2(-top) + acc_t
    out = acc[:, :HD] / acc[:, HD:]
    return out.astype(jnp.bfloat16).reshape(zq, rows, HD)


def attend_kernel(len_ref, q_ref, kv_ref, text_ref, out_ref):
    out_ref[...] = attention(len_ref, q_ref, kv_ref, text_ref)


def home_kernel(groups, inner, heads, len_ref, q_ref, kv_ref, text_ref, out_ref, stage, ss, rs):
    h, b = pl.program_id(0), pl.program_id(1)
    me = lax.axis_index("seq")
    j = lax.rem(me, inner)
    z = me // inner
    zq = q_ref.shape[0]

    @pl.when(jnp.logical_and(h == 0, b == 0))
    def _():
        greet([lax.rem(z + k, groups) * inner + j for k in range(1, groups)])

    def columns(frm, head):
        return out_ref.at[:, pl.ds(pl.multiple_of((frm * heads + head) * HD, HD), HD)]

    out = attention(len_ref, q_ref, kv_ref, text_ref)
    for n in range(zq):
        to = b * zq + n
        stage[to, h] = out[n]

        @pl.when(to != z)
        def _():
            remote(
                stage.at[to, h], columns(z, h), ss.at[to, h], rs.at[z, h], to * inner + j
            ).start()

        @pl.when(to == z)
        def _():
            pltpu.make_async_copy(stage.at[to, h], columns(z, h), ss.at[to, h]).start()

    @pl.when(jnp.logical_and(h == heads - 1, b == groups // zq - 1))
    def _():
        for head in range(heads):
            for k in range(1, groups):
                at = lax.rem(z + k, groups)
                remote(
                    stage.at[at, head], columns(at, head), ss.at[at, head], rs.at[at, head],
                    at * inner + j,
                ).wait()
            pltpu.make_async_copy(stage.at[z, head], columns(z, head), ss.at[z, head]).wait()


def attend_home(text_len, q_all, kv_all, text):
    groups, rows, width = q_all.shape
    _, _, inner, keys, _ = kv_all.shape
    heads = width // HD
    dma = pltpu.SemaphoreType.DMA
    return pl.pallas_call(
        functools.partial(home_kernel, groups, inner, heads),
        grid=(heads, groups // 2),
        in_specs=[
            pl.BlockSpec(memory_space=pltpu.SMEM),
            pl.BlockSpec((2, rows, HD), lambda h, b: (b, 0, h)),
            pl.BlockSpec((2, groups, inner, keys, HD), lambda h, b: (0, 0, 0, 0, h)),
            pl.BlockSpec((2, text.shape[1], HD), lambda h, b: (0, 0, h)),
        ],
        out_specs=ANY,
        out_shape=jax.ShapeDtypeStruct((rows, groups * width), jnp.bfloat16),
        scratch_shapes=[
            pltpu.VMEM((groups, heads, rows, HD), jnp.bfloat16),
            dma((groups, heads)),
            dma((groups, heads)),
        ],
        compiler_params=pltpu.CompilerParams(
            collective_id=2, has_side_effects=True, vmem_limit_bytes=48 << 20
        ),
    )(text_len, q_all, kv_all, text)


def attend(text_len, q_all, kv_all, text):
    qg, rows, width = q_all.shape
    _, groups, inner, keys, _ = kv_all.shape
    step = 2 if qg % 2 == 0 else 1
    return pl.pallas_call(
        attend_kernel,
        grid=(width // HD, qg // step),
        in_specs=[
            pl.BlockSpec(memory_space=pltpu.SMEM),
            pl.BlockSpec((step, rows, HD), lambda h, b: (b, 0, h)),
            pl.BlockSpec((2, groups, inner, keys, HD), lambda h, b: (0, 0, 0, 0, h)),
            pl.BlockSpec((2, text.shape[1], HD), lambda h, b: (0, 0, h)),
        ],
        out_specs=pl.BlockSpec((step, rows, HD), lambda h, b: (b, 0, h)),
        out_shape=jax.ShapeDtypeStruct(q_all.shape, jnp.bfloat16),
        compiler_params=pltpu.CompilerParams(vmem_limit_bytes=48 << 20),
    )(text_len, q_all, kv_all, text)


def pair_kernel(groups, inner, tp, in_ref, out_ref, near, far, ns, nr, fs, fr):
    me, at_tp = lax.axis_index("seq"), lax.axis_index("tp")
    z, j = me // inner, lax.rem(me, inner)
    size = inner * tp
    slot = at_tp * inner + j
    peers = []
    for k in range(1, size):
        other = lax.rem(slot + k, size)
        peers.append((other, (z * inner + lax.rem(other, inner), other // inner)))
    fars = []
    for k in range(1, groups):
        other = lax.rem(z + k, groups)
        fars.append((other, (other * inner + j, at_tp)))
    barrier = pltpu.get_barrier_semaphore()
    for _, peer in peers + fars:
        pl.semaphore_signal(barrier, inc=1, device_id=peer, device_id_type=MESH)
    pl.semaphore_wait(barrier, len(peers) + len(fars))

    def round_of(held, mine, others, send, recv):
        copies = []
        for other, peer in others:
            copy = pltpu.make_async_remote_copy(
                src_ref=held.at[mine], dst_ref=held.at[mine], send_sem=send.at[other],
                recv_sem=recv.at[mine], device_id=peer, device_id_type=MESH,
            )
            copy.start()
        for other, peer in others:
            copy = pltpu.make_async_remote_copy(
                src_ref=held.at[other], dst_ref=held.at[other], send_sem=send.at[other],
                recv_sem=recv.at[other], device_id=peer, device_id_type=MESH,
            )
            copy.wait()

    near[slot] = in_ref[...]
    round_of(near, slot, peers, ns, nr)
    far[z] = jnp.sum(near[...], axis=0)
    round_of(far, z, fars, fs, fr)
    out_ref[...] = jnp.sum(far[...], axis=0)


def pair_total(value, groups, inner):
    tp = lax.axis_size("tp")
    size = inner * tp
    dma = pltpu.SemaphoreType.DMA
    vmem = pl.BlockSpec(memory_space=pltpu.VMEM)
    return pl.pallas_call(
        functools.partial(pair_kernel, groups, inner, tp),
        in_specs=[vmem],
        out_specs=vmem,
        out_shape=jax.ShapeDtypeStruct((8, 128), jnp.float32),
        scratch_shapes=[
            pltpu.VMEM((size, 8, 128), jnp.float32),
            pltpu.VMEM((groups, 8, 128), jnp.float32),
            dma((size,)), dma((size,)), dma((groups,)), dma((groups,)),
        ],
        compiler_params=pltpu.CompilerParams(collective_id=4, has_side_effects=True),
    )(jnp.broadcast_to(value, (8, 128)))[0, 0]


def total_kernel(sizes, in_ref, out_ref, held, ss, rs):
    places = []
    for axis, size in sizes:
        me = lax.axis_index(axis)
        bit = 1
        while bit < size:
            low = lax.rem(me // bit, 2)
            places.append((axis, me + bit - 2 * bit * low))
            bit *= 2
    barrier = pltpu.get_barrier_semaphore()
    for axis, peer in places:
        pl.semaphore_signal(barrier, inc=1, device_id={axis: peer}, device_id_type=MESH)
    pl.semaphore_wait(barrier, len(places))
    out_ref[...] = in_ref[...]
    for n, (axis, peer) in enumerate(places):
        held[n, 0] = out_ref[...]
        copy = pltpu.make_async_remote_copy(
            src_ref=held.at[n, 0], dst_ref=held.at[n, 1], send_sem=ss.at[n], recv_sem=rs.at[n],
            device_id={axis: peer}, device_id_type=MESH,
        )
        copy.start()
        copy.wait()
        out_ref[...] = held[n, 0] + held[n, 1]


def total(value):
    sizes = (("seq", lax.axis_size("seq")), ("tp", lax.axis_size("tp")))
    steps = sum(size.bit_length() - 1 for _, size in sizes)
    dma = pltpu.SemaphoreType.DMA
    vmem = pl.BlockSpec(memory_space=pltpu.VMEM)
    full = jnp.broadcast_to(value, (8, 128))
    return pl.pallas_call(
        functools.partial(total_kernel, sizes),
        in_specs=[vmem],
        out_specs=vmem,
        out_shape=jax.ShapeDtypeStruct((8, 128), jnp.float32),
        scratch_shapes=[pltpu.VMEM((steps, 2, 8, 128), jnp.float32), dma((steps,)), dma((steps,))],
        compiler_params=pltpu.CompilerParams(collective_id=3, has_side_effects=True),
    )(full)[0, 0]


def shards(latents, noise, timestep, text_len, text_kv, norm_gain, w_qkv, qk_gain, w_out, out_gate):
    rows, local_width = latents.shape
    seq, tp = lax.axis_size("seq"), lax.axis_size("tp")
    at_seq, at_tp = lax.axis_index("seq"), lax.axis_index("tp")
    head_width = w_qkv.shape[2]
    heads_dev = head_width // HD
    groups = 4 if seq == 16 and heads_dev % 4 == 0 else 1
    inner = seq // groups
    width = head_width // groups

    sigma = timestep[0].astype(jnp.float32) / 1000.0
    noisy = (1.0 - sigma) * latents.astype(jnp.float32) + sigma * noise.astype(jnp.float32)
    sent = noisy.astype(jnp.bfloat16)
    if tp == 2:
        other = lax.ppermute(sent, "tp", [(0, 1), (1, 0)])
        first = jnp.where(at_tp == 0, sent, other)
        second = jnp.where(at_tp == 0, other, sent)
        full = jnp.concatenate([first, second], axis=1).astype(jnp.float32)
    else:
        full = lax.all_gather(sent, "tp", axis=1, tiled=True).astype(jnp.float32)
    center = full - jnp.mean(full, axis=-1, keepdims=True)
    spread = jnp.mean(center * center, axis=-1, keepdims=True)
    normed = (center * lax.rsqrt(spread + 1e-06) * norm_gain).astype(jnp.bfloat16)
    gains = jnp.stack(
        [qk_gain[0] * (LOG2E / HD**0.5), qk_gain[1], jnp.ones_like(qk_gain[0])]
    ).reshape(3, 1, HD)
    w = jnp.transpose(w_qkv, (1, 0, 2))
    if groups > 1:
        q_all, kv_all = deal(normed, w, gains, groups, inner)
        text = lax.dynamic_slice_in_dim(text_kv, (at_seq // inner) * width, width, 2)
        attended = attend_home(text_len, q_all, kv_all, text)
    else:
        qkv = project(normed, w, gains, groups)
        kv_all = lax.all_gather(qkv[1:, 0], "seq", axis=1)[:, None]
        attended = attend(text_len, qkv[0], kv_all, text_kv)[0]
    mixed = jnp.dot(attended, w_out, preferred_element_type=jnp.float32)
    if tp == 2:
        away = lax.dynamic_slice_in_dim(mixed, (1 - at_tp) * local_width, local_width, 1)
        away = lax.ppermute(away.astype(jnp.bfloat16), "tp", [(0, 1), (1, 0)])
        here = lax.dynamic_slice_in_dim(mixed, at_tp * local_width, local_width, 1)
        mixed = here + away.astype(jnp.float32)
    else:
        mixed = lax.psum_scatter(
            mixed.astype(jnp.bfloat16), "tp", scatter_dimension=1, tiled=True
        ).astype(jnp.float32)
    prediction = (noisy + out_gate * mixed).astype(jnp.bfloat16)
    target = noise.astype(jnp.float32) - latents.astype(jnp.float32)
    error = prediction.astype(jnp.float32) - target
    squares = jnp.sum(error * error)
    summed = pair_total(squares, groups, inner) if groups > 1 else total(squares)
    loss = summed / jnp.float32(rows * seq * local_width * tp)
    return (prediction, loss)


def solution(mesh):
    placed = (
        P("seq", "tp"),
        P("seq", "tp"),
        P(),
        P(),
        P(None, None, "tp"),
        P(),
        P(None, None, "tp"),
        P(),
        P("tp", None),
        P("tp"),
    )
    return jax.shard_map(
        shards, mesh=mesh, in_specs=placed, out_specs=(P("seq", "tp"), P()), check_vma=False
    )
```

```python
import functools

import jax
import jax.numpy as jnp
from jax import lax
from jax.experimental import pallas as pl
from jax.experimental.pallas import tpu as pltpu
from jax.sharding import PartitionSpec as P

HD = 128
MESH = pl.DeviceIdType.MESH
ANY = pl.BlockSpec(memory_space=pl.ANY)
LOG2E = 1.4426950408889634


def project_kernel(x_ref, w_ref, gain_ref, out_ref):
    part = pl.program_id(0)
    y = jnp.dot(x_ref[...], w_ref[0], preferred_element_type=jnp.float32)
    gain = gain_ref[0]
    for h in range(y.shape[1] // HD):
        block = y[:, h * HD : (h + 1) * HD]
        scale = lax.rsqrt(jnp.mean(block * block, axis=-1, keepdims=True) + 1e-06)
        scale = jnp.where(part < 2, scale, 1.0)
        out_ref[0, 0, :, h * HD : (h + 1) * HD] = (block * scale * gain).astype(jnp.bfloat16)


def project(normed, w, gains, groups):
    rows, depth = normed.shape
    width = w.shape[2] // groups
    return pl.pallas_call(
        project_kernel,
        grid=(3, groups),
        in_specs=[
            pl.BlockSpec((rows, depth), lambda s, g: (0, 0)),
            pl.BlockSpec((1, depth, width), lambda s, g: (s, 0, g)),
            pl.BlockSpec((1, 1, HD), lambda s, g: (s, 0, 0)),
        ],
        out_specs=pl.BlockSpec((1, 1, rows, width), lambda s, g: (s, g, 0, 0)),
        out_shape=jax.ShapeDtypeStruct((3, groups, rows, width), jnp.bfloat16),
        compiler_params=pltpu.CompilerParams(vmem_limit_bytes=40 << 20),
    )(normed, w, gains)


def greet(peers):
    barrier = pltpu.get_barrier_semaphore()
    for peer in peers:
        pl.semaphore_signal(barrier, inc=1, device_id={"seq": peer}, device_id_type=MESH)
    pl.semaphore_wait(barrier, len(peers))


def remote(src, dst, send, recv, peer):
    return pltpu.make_async_remote_copy(
        src_ref=src, dst_ref=dst, send_sem=send, recv_sem=recv,
        device_id={"seq": peer}, device_id_type=MESH,
    )


def group_at(i):
    return jnp.where(i == 3, 3, lax.rem(i + 1, 3))


def tile_at(t):
    keyed = t < 8
    return jnp.where(keyed, 1 + lax.rem(t, 2), 0), group_at(jnp.where(keyed, t // 2, t - 8))


def deal_kernel(
    groups, inner, x_ref, w_ref, gain_ref, q_all, kv_all,
    stage, zs, zr, xs, xr, cs, cr, fs, fr, ls,
):
    t = pl.program_id(0)
    part, to = tile_at(t)
    me = lax.axis_index("seq")
    j = lax.rem(me, inner)
    z = me // inner
    core = lax.rem(j, 2)
    x = j // 2
    xj = (1 - x) * 2 + core
    cj = x * 2 + (1 - core)
    x_mate = z * inner + xj
    c_mate = z * inner + cj

    @pl.when(t == 0)
    def _():
        greet([lax.rem(z + k, groups) * inner + j for k in range(1, groups)] + [x_mate, c_mate])

    y = jnp.dot(x_ref[...], w_ref[0], preferred_element_type=jnp.float32)
    gain = gain_ref[0]
    for h in range(y.shape[1] // HD):
        block = y[:, h * HD : (h + 1) * HD]
        scale = lax.rsqrt(jnp.mean(block * block, axis=-1, keepdims=True) + 1e-06)
        scale = jnp.where(part < 2, scale, 1.0)
        stage[part, to, :, h * HD : (h + 1) * HD] = (block * scale * gain).astype(jnp.bfloat16)

    def kv_copy(s, g, frm):
        return remote(
            stage.at[s, g], kv_all.at[s - 1, z if frm is None else frm, j], zs.at[s, g],
            zr.at[s, z if frm is None else frm], g * inner + j,
        )

    def q_copy(g, frm):
        return remote(
            stage.at[0, g], q_all.at[z if frm is None else frm], zs.at[0, g],
            zr.at[0, z if frm is None else frm], g * inner + j,
        )

    own_kv = pltpu.make_async_copy(stage.at[pl.ds(1, 2), z], kv_all.at[:, z, j], ls.at[0])
    own_q = pltpu.make_async_copy(stage.at[0, z], q_all.at[z], ls.at[1])

    @pl.when(jnp.logical_and(part > 0, to != z))
    def _():
        kv_copy(part, to, None).start()

    @pl.when(jnp.logical_and(part == 0, to != z))
    def _():
        q_copy(to, None).start()

    def spread(k):
        at = lax.rem(z + groups - k, groups)
        src = stage.at[pl.ds(1, 2), z] if k == 0 else kv_all.at[:, at, j]
        dst = kv_all.at[:, at, j]
        return (
            remote(src, dst, xs.at[k], xr.at[k], x_mate),
            remote(src, dst, cs.at[k], cr.at[k], c_mate),
        )

    @pl.when(t == 7)
    def _():
        own_kv.start()
        for copy in spread(0):
            copy.start()

    @pl.when(t == 11)
    def _():
        own_q.start()
        order = [1, 3, 2]
        for k in order:
            at = lax.rem(z + groups - k, groups)
            for s in (1, 2):
                kv_copy(s, at, at).wait_recv()
            for copy in spread(k):
                copy.start()
        passed = []
        for k in [0] + order:
            at = lax.rem(z + groups - k, groups)
            spread(k)[0].wait_recv()
            slot = kv_all.at[:, at, xj]
            passed.append(remote(slot, slot, fs.at[k], fr.at[k], c_mate))
            passed[-1].start()
        own_kv.wait()
        own_q.wait()
        for k in order:
            at = lax.rem(z + groups - k, groups)
            for s in (1, 2):
                kv_copy(s, at, at).wait_send()
            q_copy(at, at).wait()
        for k in range(groups):
            by_x, by_c = spread(k)
            by_x.wait_send()
            by_c.wait()
        for copy in passed:
            copy.wait()


def deal(normed, w, gains, groups, inner):
    rows, depth = normed.shape
    width = w.shape[2] // groups
    dma = pltpu.SemaphoreType.DMA
    return pl.pallas_call(
        functools.partial(deal_kernel, groups, inner),
        grid=(3 * groups,),
        in_specs=[
            pl.BlockSpec((rows, depth), lambda t: (0, 0)),
            pl.BlockSpec((1, depth, width), lambda t: (tile_at(t)[0], 0, tile_at(t)[1])),
            pl.BlockSpec((1, 1, HD), lambda t: (tile_at(t)[0], 0, 0)),
        ],
        out_specs=[ANY, ANY],
        out_shape=[
            jax.ShapeDtypeStruct((groups, rows, width), jnp.bfloat16),
            jax.ShapeDtypeStruct((2, groups, inner, rows, width), jnp.bfloat16),
        ],
        scratch_shapes=[
            pltpu.VMEM((3, groups, rows, width), jnp.bfloat16), dma((3, 4)), dma((3, 4)),
        ]
        + [dma((4,)) for _ in range(6)]
        + [dma((2,))],
        compiler_params=pltpu.CompilerParams(
            collective_id=1, has_side_effects=True, vmem_limit_bytes=40 << 20
        ),
    )(normed, w, gains)


def attention(len_ref, q_ref, kv_ref, text_ref):
    zq, rows, _ = q_ref.shape
    q = q_ref[...].reshape(zq * rows, HD)
    nt = (((1,), (1,)), ((), ()))
    text = text_ref.shape[1]
    ones = jnp.ones((text, HD), jnp.bfloat16)
    st = lax.dot_general(q, text_ref[0], nt, preferred_element_type=jnp.float32)
    ok = lax.broadcasted_iota(jnp.int32, st.shape, 1) < len_ref[0]
    st = jnp.where(ok, st, -1e30)
    top = jnp.maximum(jnp.max(st, axis=-1, keepdims=True), 0.0)
    pt = jnp.exp2(st - top).astype(jnp.bfloat16)
    acc_t = jnp.dot(
        pt, jnp.concatenate([text_ref[1], ones], axis=1), preferred_element_type=jnp.float32
    )
    _, groups, inner, keys, _ = kv_ref.shape
    ones = jnp.ones((2 * keys, HD), jnp.bfloat16)
    acc = jnp.zeros((zq * rows, 2 * HD), jnp.float32)
    for g in range(groups):
        for i in range(0, inner, 2):
            k = kv_ref[0, g, i : i + 2].reshape(2 * keys, HD)
            v = kv_ref[1, g, i : i + 2].reshape(2 * keys, HD)
            s = lax.dot_general(q, k, nt, preferred_element_type=jnp.float32)
            p = jnp.exp2(s).astype(jnp.bfloat16)
            acc += jnp.dot(
                p, jnp.concatenate([v, ones], axis=1), preferred_element_type=jnp.float32
            )
    acc = acc * jnp.exp2(-top) + acc_t
    out = acc[:, :HD] / acc[:, HD:]
    return out.astype(jnp.bfloat16).reshape(zq, rows, HD)


def attend_kernel(len_ref, q_ref, kv_ref, text_ref, out_ref):
    out_ref[...] = attention(len_ref, q_ref, kv_ref, text_ref)


def home_kernel(groups, inner, heads, len_ref, q_ref, kv_ref, text_ref, out_ref, stage, ss, rs):
    h, b = pl.program_id(0), pl.program_id(1)
    me = lax.axis_index("seq")
    j = lax.rem(me, inner)
    z = me // inner
    zq = q_ref.shape[0]

    @pl.when(jnp.logical_and(h == 0, b == 0))
    def _():
        greet([lax.rem(z + k, groups) * inner + j for k in range(1, groups)])

    def columns(frm, head):
        return out_ref.at[:, pl.ds(pl.multiple_of((frm * heads + head) * HD, HD), HD)]

    out = attention(len_ref, q_ref, kv_ref, text_ref)
    for n in range(zq):
        to = b * zq + n
        stage[to, h] = out[n]

        @pl.when(to != z)
        def _():
            remote(
                stage.at[to, h], columns(z, h), ss.at[to, h], rs.at[z, h], to * inner + j
            ).start()

        @pl.when(to == z)
        def _():
            pltpu.make_async_copy(stage.at[to, h], columns(z, h), ss.at[to, h]).start()

    @pl.when(jnp.logical_and(h == heads - 1, b == groups // zq - 1))
    def _():
        for head in range(heads):
            for k in range(1, groups):
                at = lax.rem(z + k, groups)
                remote(
                    stage.at[at, head], columns(at, head), ss.at[at, head], rs.at[at, head],
                    at * inner + j,
                ).wait()
            pltpu.make_async_copy(stage.at[z, head], columns(z, head), ss.at[z, head]).wait()


def attend_home(text_len, q_all, kv_all, text):
    groups, rows, width = q_all.shape
    _, _, inner, keys, _ = kv_all.shape
    heads = width // HD
    dma = pltpu.SemaphoreType.DMA
    return pl.pallas_call(
        functools.partial(home_kernel, groups, inner, heads),
        grid=(heads, groups // 2),
        in_specs=[
            pl.BlockSpec(memory_space=pltpu.SMEM),
            pl.BlockSpec((2, rows, HD), lambda h, b: (b, 0, h)),
            pl.BlockSpec((2, groups, inner, keys, HD), lambda h, b: (0, 0, 0, 0, h)),
            pl.BlockSpec((2, text.shape[1], HD), lambda h, b: (0, 0, h)),
        ],
        out_specs=ANY,
        out_shape=jax.ShapeDtypeStruct((rows, groups * width), jnp.bfloat16),
        scratch_shapes=[
            pltpu.VMEM((groups, heads, rows, HD), jnp.bfloat16),
            dma((groups, heads)),
            dma((groups, heads)),
        ],
        compiler_params=pltpu.CompilerParams(
            collective_id=2, has_side_effects=True, vmem_limit_bytes=48 << 20
        ),
    )(text_len, q_all, kv_all, text)


def attend(text_len, q_all, kv_all, text):
    qg, rows, width = q_all.shape
    _, groups, inner, keys, _ = kv_all.shape
    step = 2 if qg % 2 == 0 else 1
    return pl.pallas_call(
        attend_kernel,
        grid=(width // HD, qg // step),
        in_specs=[
            pl.BlockSpec(memory_space=pltpu.SMEM),
            pl.BlockSpec((step, rows, HD), lambda h, b: (b, 0, h)),
            pl.BlockSpec((2, groups, inner, keys, HD), lambda h, b: (0, 0, 0, 0, h)),
            pl.BlockSpec((2, text.shape[1], HD), lambda h, b: (0, 0, h)),
        ],
        out_specs=pl.BlockSpec((step, rows, HD), lambda h, b: (b, 0, h)),
        out_shape=jax.ShapeDtypeStruct(q_all.shape, jnp.bfloat16),
        compiler_params=pltpu.CompilerParams(vmem_limit_bytes=48 << 20),
    )(text_len, q_all, kv_all, text)


def pair_kernel(groups, inner, tp, in_ref, out_ref, near, far, ns, nr, fs, fr):
    me, at_tp = lax.axis_index("seq"), lax.axis_index("tp")
    z, j = me // inner, lax.rem(me, inner)
    size = inner * tp
    slot = at_tp * inner + j
    peers = []
    for k in range(1, size):
        other = lax.rem(slot + k, size)
        peers.append((other, (z * inner + lax.rem(other, inner), other // inner)))
    fars = []
    for k in range(1, groups):
        other = lax.rem(z + k, groups)
        fars.append((other, (other * inner + j, at_tp)))
    barrier = pltpu.get_barrier_semaphore()
    for _, peer in peers + fars:
        pl.semaphore_signal(barrier, inc=1, device_id=peer, device_id_type=MESH)
    pl.semaphore_wait(barrier, len(peers) + len(fars))

    def round_of(held, mine, others, send, recv):
        copies = []
        for other, peer in others:
            copy = pltpu.make_async_remote_copy(
                src_ref=held.at[mine], dst_ref=held.at[mine], send_sem=send.at[other],
                recv_sem=recv.at[mine], device_id=peer, device_id_type=MESH,
            )
            copy.start()
        for other, peer in others:
            copy = pltpu.make_async_remote_copy(
                src_ref=held.at[other], dst_ref=held.at[other], send_sem=send.at[other],
                recv_sem=recv.at[other], device_id=peer, device_id_type=MESH,
            )
            copy.wait()

    near[slot] = in_ref[...]
    round_of(near, slot, peers, ns, nr)
    far[z] = jnp.sum(near[...], axis=0)
    round_of(far, z, fars, fs, fr)
    out_ref[...] = jnp.sum(far[...], axis=0)


def pair_total(value, groups, inner):
    tp = lax.axis_size("tp")
    size = inner * tp
    dma = pltpu.SemaphoreType.DMA
    vmem = pl.BlockSpec(memory_space=pltpu.VMEM)
    return pl.pallas_call(
        functools.partial(pair_kernel, groups, inner, tp),
        in_specs=[vmem],
        out_specs=vmem,
        out_shape=jax.ShapeDtypeStruct((8, 128), jnp.float32),
        scratch_shapes=[
            pltpu.VMEM((size, 8, 128), jnp.float32),
            pltpu.VMEM((groups, 8, 128), jnp.float32),
            dma((size,)), dma((size,)), dma((groups,)), dma((groups,)),
        ],
        compiler_params=pltpu.CompilerParams(collective_id=4, has_side_effects=True),
    )(jnp.broadcast_to(value, (8, 128)))[0, 0]


def total_kernel(sizes, in_ref, out_ref, held, ss, rs):
    places = []
    for axis, size in sizes:
        me = lax.axis_index(axis)
        bit = 1
        while bit < size:
            low = lax.rem(me // bit, 2)
            places.append((axis, me + bit - 2 * bit * low))
            bit *= 2
    barrier = pltpu.get_barrier_semaphore()
    for axis, peer in places:
        pl.semaphore_signal(barrier, inc=1, device_id={axis: peer}, device_id_type=MESH)
    pl.semaphore_wait(barrier, len(places))
    out_ref[...] = in_ref[...]
    for n, (axis, peer) in enumerate(places):
        held[n, 0] = out_ref[...]
        copy = pltpu.make_async_remote_copy(
            src_ref=held.at[n, 0], dst_ref=held.at[n, 1], send_sem=ss.at[n], recv_sem=rs.at[n],
            device_id={axis: peer}, device_id_type=MESH,
        )
        copy.start()
        copy.wait()
        out_ref[...] = held[n, 0] + held[n, 1]


def total(value):
    sizes = (("seq", lax.axis_size("seq")), ("tp", lax.axis_size("tp")))
    steps = sum(size.bit_length() - 1 for _, size in sizes)
    dma = pltpu.SemaphoreType.DMA
    vmem = pl.BlockSpec(memory_space=pltpu.VMEM)
    full = jnp.broadcast_to(value, (8, 128))
    return pl.pallas_call(
        functools.partial(total_kernel, sizes),
        in_specs=[vmem],
        out_specs=vmem,
        out_shape=jax.ShapeDtypeStruct((8, 128), jnp.float32),
        scratch_shapes=[pltpu.VMEM((steps, 2, 8, 128), jnp.float32), dma((steps,)), dma((steps,))],
        compiler_params=pltpu.CompilerParams(collective_id=3, has_side_effects=True),
    )(full)[0, 0]


def shards(latents, noise, timestep, text_len, text_kv, norm_gain, w_qkv, qk_gain, w_out, out_gate):
    rows, local_width = latents.shape
    seq, tp = lax.axis_size("seq"), lax.axis_size("tp")
    at_seq, at_tp = lax.axis_index("seq"), lax.axis_index("tp")
    head_width = w_qkv.shape[2]
    heads_dev = head_width // HD
    groups = 4 if seq == 16 and heads_dev % 4 == 0 else 1
    inner = seq // groups
    width = head_width // groups

    sigma = timestep[0].astype(jnp.float32) / 1000.0
    noisy = (1.0 - sigma) * latents.astype(jnp.float32) + sigma * noise.astype(jnp.float32)
    sent = noisy.astype(jnp.bfloat16)
    if tp == 2:
        other = lax.ppermute(sent, "tp", [(0, 1), (1, 0)])
        first = jnp.where(at_tp == 0, sent, other)
        second = jnp.where(at_tp == 0, other, sent)
        full = jnp.concatenate([first, second], axis=1).astype(jnp.float32)
    else:
        full = lax.all_gather(sent, "tp", axis=1, tiled=True).astype(jnp.float32)
    center = full - jnp.mean(full, axis=-1, keepdims=True)
    spread = jnp.mean(center * center, axis=-1, keepdims=True)
    normed = (center * lax.rsqrt(spread + 1e-06) * norm_gain).astype(jnp.bfloat16)
    gains = jnp.stack(
        [qk_gain[0] * (LOG2E / HD**0.5), qk_gain[1], jnp.ones_like(qk_gain[0])]
    ).reshape(3, 1, HD)
    w = jnp.transpose(w_qkv, (1, 0, 2))
    if groups > 1:
        q_all, kv_all = deal(normed, w, gains, groups, inner)
        text = lax.dynamic_slice_in_dim(text_kv, (at_seq // inner) * width, width, 2)
        attended = attend_home(text_len, q_all, kv_all, text)
    else:
        qkv = project(normed, w, gains, groups)
        kv_all = lax.all_gather(qkv[1:, 0], "seq", axis=1)[:, None]
        attended = attend(text_len, qkv[0], kv_all, text_kv)[0]
    if tp == 2:
        half = rows // 2
        parts = []
        for at in (0, half):
            part = jnp.dot(attended[at : at + half], w_out, preferred_element_type=jnp.float32)
            low, high = part[:, :local_width], part[:, local_width:]
            away = jnp.where(at_tp == 0, high, low).astype(jnp.bfloat16)
            away = lax.ppermute(away, "tp", [(0, 1), (1, 0)])
            parts.append(jnp.where(at_tp == 0, low, high) + away.astype(jnp.float32))
        mixed = jnp.concatenate(parts, axis=0)
    else:
        mixed = jnp.dot(attended, w_out, preferred_element_type=jnp.float32)
        mixed = lax.psum_scatter(
            mixed.astype(jnp.bfloat16), "tp", scatter_dimension=1, tiled=True
        ).astype(jnp.float32)
    prediction = (noisy + out_gate * mixed).astype(jnp.bfloat16)
    target = noise.astype(jnp.float32) - latents.astype(jnp.float32)
    error = prediction.astype(jnp.float32) - target
    squares = jnp.sum(error * error)
    summed = pair_total(squares, groups, inner) if groups > 1 else total(squares)
    loss = summed / jnp.float32(rows * seq * local_width * tp)
    return (prediction, loss)


def solution(mesh):
    placed = (
        P("seq", "tp"),
        P("seq", "tp"),
        P(),
        P(),
        P(None, None, "tp"),
        P(),
        P(None, None, "tp"),
        P(),
        P("tp", None),
        P("tp"),
    )
    return jax.shard_map(
        shards, mesh=mesh, in_specs=placed, out_specs=(P("seq", "tp"), P()), check_vma=False
    )
```
